512 devices in a mesh: row: 16 (over y_lo, x, core), col: 32 (over z, y_hi).
Axes of the slice: x: 4, y: 8 (y_hi: 4, y_lo: 2; y = y_hi * 2 + y_lo), z: 8, core: 2. Of those that a mesh axis runs over, the one named last changes fastest.
Arguments:
- panel_adjoint: float32 [24576, 512], P('row', 'col'), may hold values from -6 to 6
- panel_factor: float32 [24576, 512], P('row', 'col'), may hold values from -0.0390625 to 0.0390625
- diag_inverse: float32 [512, 512], P('row', 'col'), as said below
- head_factor: float32 [512, 8192], P('row', 'col'), may hold values from -0.25 to 0.25
- below_factor: float32 [24576, 8192], P('row', 'col'), may hold values from -0.0390625 to 0.0390625
- diag_adjoint: float32 [512, 512], P('row', 'col'), may hold values from -6 to 6
- head_adjoint: float32 [512, 8192], P('row', 'col'), may hold values from -6 to 6
- below_adjoint: float32 [24576, 8192], P('row', 'col'), may hold values from -6 to 6
Outputs:
- diag_updated: float32 [512, 512], P('row', 'col')
- head_updated: float32 [512, 8192], P('row', 'col')
- below_updated: float32 [24576, 8192], P('row', 'col')
The draws below stay inside these ranges and needn't reach their ends.
Inputs may be any that keep to these rules, and one draw needn't show every extreme that they name: `diag_inverse`: upper triangular with a positive diagonal.
All inputs are finite; a program needn't handle non-finite values.
Results may differ from the reference program's by a relative error of at most 0.000084.
Values sent between devices are 32-bit elements; how exact they have to be, the bound alone decides.
No kernel may reach another device: no remote copies, remote signals or barrier semaphores. Data moves between devices by JAX's collectives and lax.ppermute only.
A program may use at most 64 MiB of HBM per device.

```python
import jax
import jax.numpy as jnp
from jax import lax

NB = 512
M = 24576
K = 8192


def draw_diag_inverse(key, part):
    key_off, key_diag = jax.random.split(key)
    index = jnp.arange(NB)
    upper = (index[None, :] > index[:, None]).astype(jnp.float32)
    off_part = jax.random.normal(key_off, (NB, NB), jnp.float32) * 0.05 * upper
    diag_part = jax.random.uniform(key_diag, (NB,), jnp.float32, 1.0, 2.0)
    return off_part + jnp.diag(diag_part)


def shard_levels(key, shape, cuts, least, largest):
    def one(position, blocks):
        steps = jax.random.uniform(jax.random.fold_in(jax.random.fold_in(key, 6), position), (blocks,), jnp.float32, least / len(cuts), largest / len(cuts))
        return jnp.repeat(jnp.exp(steps), shape[position] // blocks).reshape((-1,) + (1,) * (len(shape) - position - 1))

    loudness = one(*cuts[0])
    for cut in cuts[1:]:
        loudness = loudness * one(*cut)
    return loudness


def normal_values(key, dims, width, bound, cuts=(), dtype=jnp.bfloat16):
    entries = jax.random.normal(key, dims, jnp.float32) * width
    if len(cuts) > 0:
        entries = shard_levels(key, dims, cuts, -0.22, 0.18) * entries
    return jnp.clip(entries, min=-bound, max=bound).astype(dtype)


def setup_inputs(seed: int = 0) -> dict:
    key_list = jax.random.split(jax.random.key(seed), 9)
    panel_adjoint = normal_values(key_list[0], (M, NB), 1.0, 6.0, ((0, 16), (1, 32)), jnp.float32)
    panel_factor = normal_values(key_list[1], (M, NB), M ** -0.5, 0.0390625, ((0, 16), (1, 32)), jnp.float32)
    diag_inverse = draw_diag_inverse(jax.random.fold_in(key_list[8], 71), 0)
    head_factor = normal_values(key_list[3], (NB, K), NB ** -0.5, 0.25, ((0, 16), (1, 32)), jnp.float32)
    below_factor = normal_values(key_list[4], (M, K), M ** -0.5, 0.0390625, ((0, 16), (1, 32)), jnp.float32)
    diag_adjoint = normal_values(key_list[5], (NB, NB), 1.0, 6.0, ((0, 16), (1, 32)), jnp.float32)
    head_adjoint = normal_values(key_list[6], (NB, K), 1.0, 6.0, ((0, 16), (1, 32)), jnp.float32)
    below_adjoint = normal_values(key_list[7], (M, K), 1.0, 6.0, ((0, 16), (1, 32)), jnp.float32)
    return {"panel_adjoint": panel_adjoint, "panel_factor": panel_factor, "diag_inverse": diag_inverse, "head_factor": head_factor, "below_factor": below_factor, "diag_adjoint": diag_adjoint, "head_adjoint": head_adjoint, "below_adjoint": below_adjoint}


def mult(left, right):
    return jnp.dot(left, right, preferred_element_type=jnp.float32, precision=lax.Precision.HIGHEST)


def tmult(left, right):
    return lax.dot_general(left, right, (((0,), (0,)), ((), ())), preferred_element_type=jnp.float32, precision=lax.Precision.HIGHEST)


def reference(panel_adjoint, panel_factor, diag_inverse, head_factor, below_factor, diag_adjoint, head_adjoint, below_adjoint):
    solved = mult(panel_adjoint, diag_inverse)
    diag_updated = diag_adjoint - tmult(solved, panel_factor)
    head_updated = head_adjoint - tmult(solved, below_factor)
    below_updated = below_adjoint - mult(solved, head_factor)
    return diag_updated, head_updated, below_updated
```

```python
import jax
import jax.numpy as jnp
from jax import lax
from jax.sharding import PartitionSpec as P

ZS = 8
YS = 4


def col_groups():
    near = [[z * YS + h for h in range(YS)] for z in range(ZS)]
    far = [[z * YS + h for z in range(ZS)] for h in range(YS)]
    return near, far


def dot(left, right, dims):
    return lax.dot_general(
        left,
        right,
        (dims, ((), ())),
        preferred_element_type=jnp.float32,
        precision=lax.Precision.HIGH,
    )


def spread(block, axis, groups, size):
    copies = jnp.broadcast_to(block[None], (size,) + block.shape)
    got = lax.all_to_all(copies, axis, 0, 0, tiled=True, axis_index_groups=groups)
    return got.reshape((size * block.shape[0],) + block.shape[1:])


def on_device(
    panel_adjoint,
    panel_factor,
    diag_inverse,
    head_factor,
    below_factor,
    diag_adjoint,
    head_adjoint,
    below_adjoint,
):
    near, far = col_groups()
    rows = head_factor.shape[0]
    width = head_factor.shape[1]
    part = spread(panel_adjoint.T, "col", near, YS)
    part, inverse = lax.optimization_barrier((part, diag_inverse.T))
    panel = lax.all_gather(part, "col", axis=0, tiled=True, axis_index_groups=far)
    inverse = spread(spread(inverse, "col", near, YS), "col", far, ZS)
    packed = spread(jnp.concatenate([head_factor, inverse.T], 1), "row", None, 16)
    head_whole, inverse = packed[:, :width], packed[:, width:]
    weight = dot(inverse, head_whole, ((1,), (0,)))
    factors = jnp.concatenate([below_factor, panel_factor], 1)
    panel, weight, factors = lax.optimization_barrier((panel, weight, factors))
    term = dot(panel, factors, ((1,), (0,)))
    term = dot(inverse, term, ((0,), (0,)))
    parts = lax.all_to_all(term.reshape(16, rows, -1), "row", 0, 0, tiled=True)
    below_updated = below_adjoint - dot(panel, weight, ((0,), (0,)))
    total = parts.sum(0)
    head_updated = head_adjoint - total[:, :width]
    diag_updated = diag_adjoint - total[:, width:]
    return (diag_updated, head_updated, below_updated)


def solution(mesh):
    placed = (P("row", "col"),) * 8
    return jax.shard_map(
        on_device,
        mesh=mesh,
        in_specs=placed,
        out_specs=(P("row", "col"),) * 3,
        check_vma=False,
    )
```

```python
import functools

import jax
import jax.numpy as jnp
from jax import lax
from jax.experimental import pallas as pl
from jax.experimental.pallas import tpu as pltpu
from jax.sharding import PartitionSpec as P

ZS = 8
YS = 4
RS = 16
TILE = 256
FLOPS = 20 * 10**10
VMEM = 14 * 2**20


def col_groups():
    near = [[z * YS + h for h in range(YS)] for z in range(ZS)]
    far = [[z * YS + h for z in range(ZS)] for h in range(YS)]
    return near, far


def z_shift(step):
    return [(z * YS + h, ((z + step) % ZS) * YS + h) for z in range(ZS) for h in range(YS)]


def spread(block, axis, groups, size):
    copies = jnp.broadcast_to(block[None], (size,) + block.shape)
    return lax.all_to_all(copies, axis, 0, 0, tiled=True, axis_index_groups=groups)


def split(x):
    high = x.astype(jnp.bfloat16)
    return high, (x - high.astype(jnp.float32)).astype(jnp.bfloat16)


def dot3(left, right, dims):
    def one(a, b):
        return lax.dot_general(a, b, (dims, ((), ())), preferred_element_type=jnp.float32)

    return one(left[0], right[0]) + (one(left[0], right[1]) + one(left[1], right[0]))


def joined(refs):
    return jnp.concatenate([r[...] for r in refs], 0) if len(refs) > 1 else refs[0][...]


def products(pieces, b_ref, f_ref):
    piece = split(pieces)
    return dot3(piece, split(b_ref[...]), ((1,), (0,))), dot3(piece, split(f_ref[...]), ((1,), (1,)))


def term_kernel(count, *refs):
    b_ref, f_ref, t_ref, s_ref = refs[count:]
    t_ref[...], s_ref[...] = products(joined(refs[:count]), b_ref, f_ref)


def params(**more):
    return pltpu.CompilerParams(vmem_limit_bytes=VMEM, **more)


def terms(pieces, b, f):
    rows = sum(p.shape[0] for p in pieces)
    return pl.pallas_call(
        functools.partial(term_kernel, len(pieces)),
        out_shape=(
            jax.ShapeDtypeStruct((rows, b.shape[1]), jnp.float32),
            jax.ShapeDtypeStruct((rows, f.shape[0]), jnp.float32),
        ),
        compiler_params=params(),
        cost_estimate=pl.CostEstimate(flops=FLOPS, bytes_accessed=0, transcendentals=0),
        name="terms",
    )(*pieces, b, f)


def weight_kernel(width, packed_ref, w_ref, high_ref, low_ref):
    inverse = packed_ref[:, width:]
    w_ref[...] = dot3(split(inverse), split(packed_ref[:, :width]), ((1,), (0,)))
    high_ref[...], low_ref[...] = split(inverse.T)


def weights(packed, width):
    nb = packed.shape[0]
    return pl.pallas_call(
        functools.partial(weight_kernel, width),
        out_shape=(
            jax.ShapeDtypeStruct((nb, width), jnp.float32),
            jax.ShapeDtypeStruct((nb, nb), jnp.bfloat16),
            jax.ShapeDtypeStruct((nb, nb), jnp.bfloat16),
        ),
        compiler_params=params(),
        cost_estimate=pl.CostEstimate(flops=10**9, bytes_accessed=0, transcendentals=0),
        name="weights",
    )(packed)


def head_kernel(group, z_ref, *refs):
    up_ref, down_ref, b_ref, f_ref, high_ref, low_ref = refs[:6]
    found = refs[6:14]
    out_ref, t_scr, s_scr = refs[14:]
    z = z_ref[0]

    def place(offset):
        return pl.ds(pl.multiple_of(lax.rem(z + offset + ZS, ZS) * group, group), group)

    for step in range(ZS // 2):
        t_ref, s_ref = found[2 * step], found[2 * step + 1]
        for part, offset in enumerate((0,) if step == 0 else (-step, step)):
            t_scr[place(offset), :] = t_ref[part * group : (part + 1) * group, :]
            s_scr[place(offset), :] = s_ref[part * group : (part + 1) * group, :]
    last = place(ZS // 2)
    t_scr[last, :], s_scr[last, :] = products(joined((up_ref, down_ref)), b_ref, f_ref)
    turned = (high_ref[...], low_ref[...])
    head = dot3(turned, split(t_scr[...]), ((1,), (0,)))
    diag = dot3(turned, split(s_scr[...]), ((1,), (0,)))
    rows = head.shape[0] // RS
    small = diag.shape[1]
    for r in range(RS):
        out_ref[r, :rows, :] = head[r * rows : (r + 1) * rows]
        for q in range(rows // 8):
            out_ref[r, rows:, q * 64 : q * 64 + small] = diag[r * rows + q * 8 : r * rows + q * 8 + 8]


def head_terms(z, up, down, b, f, turned, found):
    nb = turned[0].shape[0]
    width, small = b.shape[1], f.shape[0]
    args = (up, down, b, f) + turned + found
    return pl.pallas_call(
        functools.partial(head_kernel, nb // ZS),
        out_shape=jax.ShapeDtypeStruct((RS, nb // RS + 8, width), jnp.float32),
        in_specs=[pl.BlockSpec(memory_space=pltpu.SMEM)]
        + [pl.BlockSpec(memory_space=pltpu.VMEM)] * len(args),
        out_specs=pl.BlockSpec(memory_space=pltpu.VMEM),
        scratch_shapes=[pltpu.VMEM((nb, width), jnp.float32), pltpu.VMEM((nb, small), jnp.float32)],
        compiler_params=params(),
        cost_estimate=pl.CostEstimate(flops=10**9, bytes_accessed=0, transcendentals=0),
        name="head_terms",
    )(z, *args)


def below_kernel(group, z_ref, *refs):
    pieces, (w_ref, old_ref, new_ref) = refs[:9], refs[9:]
    z = z_ref[0]
    order = (0, -1, 1, -2, 2, -3, 3, 4)
    weight = jnp.concatenate(
        [
            w_ref[pl.ds(pl.multiple_of(lax.rem(z + k + ZS, ZS) * group, group), group), :]
            for k in order
        ],
        0,
    )
    panel = joined(pieces)
    new_ref[...] = old_ref[...] - dot3(split(panel), split(weight), ((0,), (0,)))


def below_update(z, pieces, weight, old):
    length, width = old.shape
    nb = weight.shape[0]
    return pl.pallas_call(
        functools.partial(below_kernel, nb // ZS),
        grid=(length // TILE,),
        out_shape=jax.ShapeDtypeStruct(old.shape, jnp.float32),
        in_specs=[pl.BlockSpec(memory_space=pltpu.SMEM)]
        + [pl.BlockSpec((p.shape[0], TILE), lambda i: (0, i)) for p in pieces]
        + [
            pl.BlockSpec((nb, width), lambda i: (0, 0)),
            pl.BlockSpec((TILE, width), lambda i: (i, 0)),
        ],
        out_specs=pl.BlockSpec((TILE, width), lambda i: (i, 0)),
        compiler_params=params(),
        cost_estimate=pl.CostEstimate(flops=6 * length * nb * width, bytes_accessed=0, transcendentals=0),
        name="below_update",
    )(z, *pieces, weight, old)


def finish_kernel(parts_ref, head_ref, diag_ref, new_head_ref, new_diag_ref):
    rows = head_ref.shape[0]
    small = diag_ref.shape[0]
    total = parts_ref[0]
    for r in range(1, RS):
        total = total + parts_ref[r]
    new_head_ref[...] = head_ref[...] - total[:rows]
    tail = total[rows:]
    diag = jnp.concatenate([tail[:, q * 64 : q * 64 + small] for q in range(rows // 8)], 0)
    new_diag_ref[...] = diag_ref[...] - diag.T


def finish(parts, head, diag):
    return pl.pallas_call(
        finish_kernel,
        out_shape=(
            jax.ShapeDtypeStruct(head.shape, jnp.float32),
            jax.ShapeDtypeStruct(diag.shape, jnp.float32),
        ),
        compiler_params=params(),
        name="finish",
    )(parts, head, diag)


def on_device(
    panel_adjoint,
    panel_factor,
    diag_inverse,
    head_factor,
    below_factor,
    diag_adjoint,
    head_adjoint,
    below_adjoint,
):
    near, far = col_groups()
    z = (lax.axis_index("col") // YS).astype(jnp.int32).reshape(1)
    rows, width = head_factor.shape
    length, cols = panel_adjoint.shape
    nb = cols * ZS * YS
    group = cols * YS
    factor = panel_factor.T
    corner = jnp.pad(diag_inverse.T, ((0, 0), (0, 128 - rows)))
    part = spread(jnp.concatenate([panel_adjoint.T, corner], 1), "col", near, YS)
    part = part.reshape(group, length + 128)
    up = down = part[:, :length]
    pieces = [up]
    found = terms((up,), below_factor, factor)
    for step in range(1, ZS // 2):
        up = lax.ppermute(up, "col", z_shift(1))
        down = lax.ppermute(down, "col", z_shift(-1))
        found += tuple(terms((up, down), below_factor, factor))
        pieces += [up, down]
    up = lax.ppermute(up[: group // 2], "col", z_shift(1))
    down = lax.ppermute(down[group // 2 :], "col", z_shift(-1))
    pieces += [up, down]
    inverse = spread(part[:, length:], "col", far, ZS).reshape(nb, 128)[:, :rows]
    packed = spread(jnp.concatenate([head_factor, inverse.T], 1), "row", None, RS)
    weight, high, low = weights(packed.reshape(nb, width + nb), width)
    local = head_terms(z, up, down, below_factor, factor, (high, low), tuple(found))
    parts = lax.all_to_all(local, "row", 0, 0, tiled=True)
    below_updated = below_update(z, pieces, weight, below_adjoint)
    head_updated, diag_updated = finish(parts, head_adjoint, diag_adjoint.T)
    return (diag_updated.T, head_updated, below_updated)


def solution(mesh):
    placed = (P("row", "col"),) * 8
    return jax.shard_map(
        on_device,
        mesh=mesh,
        in_specs=placed,
        out_specs=(P("row", "col"),) * 3,
        check_vma=False,
    )
```

```python
import functools

import jax
import jax.numpy as jnp
from jax import lax
from jax.experimental import pallas as pl
from jax.experimental.pallas import tpu as pltpu
from jax.sharding import PartitionSpec as P

ZS = 8
YS = 4
RS = 16
TILE = 256
COSTS = (2 * 10**11,) * 4
VMEM = 14 * 2**20


def col_groups():
    near = [[z * YS + h for h in range(YS)] for z in range(ZS)]
    far = [[z * YS + h for z in range(ZS)] for h in range(YS)]
    return near, far


def along_z(step):
    moves = []
    for r in range(RS):
        for z in range(ZS):
            to = (z + (step if r % 2 == 0 else -step)) % ZS
            moves += [((r * ZS + z) * YS + h, (r * ZS + to) * YS + h) for h in range(YS)]
    return moves


def exchange(copies, axis, groups):
    return lax.all_to_all(copies, axis, 0, 0, tiled=True, axis_index_groups=groups)


def split(x):
    high = x.astype(jnp.bfloat16)
    return high, (x - high.astype(jnp.float32)).astype(jnp.bfloat16)


def dot3(left, right, dims):
    def one(a, b):
        return lax.dot_general(a, b, (dims, ((), ())), preferred_element_type=jnp.float32)

    return one(left[0], right[0]) + (one(left[0], right[1]) + one(left[1], right[0]))


def joined(refs):
    return jnp.concatenate([r[...] for r in refs], 0) if len(refs) > 1 else refs[0][...]


def products(pieces, b_ref, f_ref):
    piece = split(pieces)
    return dot3(piece, split(b_ref[...]), ((1,), (0,))), dot3(piece, split(f_ref[...]), ((1,), (1,)))


def term_kernel(count, *refs):
    b_ref, f_ref, t_ref, s_ref = refs[count:]
    t_ref[...], s_ref[...] = products(joined(refs[:count]), b_ref, f_ref)


def params(**more):
    return pltpu.CompilerParams(vmem_limit_bytes=VMEM, **more)


def terms(pieces, b, f, cost):
    rows = sum(p.shape[0] for p in pieces)
    return pl.pallas_call(
        functools.partial(term_kernel, len(pieces)),
        out_shape=(
            jax.ShapeDtypeStruct((rows, b.shape[1]), jnp.float32),
            jax.ShapeDtypeStruct((rows, f.shape[0]), jnp.float32),
        ),
        compiler_params=params(),
        cost_estimate=pl.CostEstimate(flops=cost, bytes_accessed=0, transcendentals=0),
        name="terms",
    )(*pieces, b, f)


def weight_kernel(width, packed_ref, w_ref):
    inverse = split(packed_ref[:, width:])
    w_ref[...] = dot3(inverse, split(packed_ref[:, :width]), ((1,), (0,)))


def weights(packed, width):
    nb = packed.shape[0]
    return pl.pallas_call(
        functools.partial(weight_kernel, width),
        out_shape=jax.ShapeDtypeStruct((nb, width), jnp.float32),
        compiler_params=params(),
        cost_estimate=pl.CostEstimate(flops=10**9, bytes_accessed=0, transcendentals=0),
        name="weights",
    )(packed)


def position(z_ref, offset, group):
    place = lax.rem(z_ref[0] + offset * z_ref[1] + ZS, ZS)
    return pl.ds(pl.multiple_of(place * group, group), group)


def head_kernel(group, z_ref, *refs):
    piece_ref, b_ref, f_ref, packed_ref = refs[:4]
    found = refs[4:12]
    out_ref, t_scr, s_scr = refs[12:]
    turned = split(packed_ref[:, b_ref.shape[1] :].T)
    for step in range(ZS // 2):
        t_ref, s_ref = found[2 * step], found[2 * step + 1]
        for part, offset in enumerate((0,) if step == 0 else (step, -step)):
            place = position(z_ref, offset, group)
            t_scr[place, :] = t_ref[part * group : (part + 1) * group, :]
            s_scr[place, :] = s_ref[part * group : (part + 1) * group, :]
    last = position(z_ref, ZS // 2, group)
    t_scr[last, :], s_scr[last, :] = products(piece_ref[...], b_ref, f_ref)
    head = dot3(turned, split(t_scr[...]), ((1,), (0,)))
    diag = dot3(turned, split(s_scr[...]), ((1,), (0,)))
    rows = head.shape[0] // RS
    small = diag.shape[1]
    for r in range(RS):
        out_ref[r, :rows, :] = head[r * rows : (r + 1) * rows]
        for q in range(rows // 8):
            out_ref[r, rows:, q * 64 : q * 64 + small] = diag[r * rows + q * 8 : r * rows + q * 8 + 8]


def head_terms(z, piece, b, f, packed, found):
    nb = packed.shape[0]
    width, small = b.shape[1], f.shape[0]
    args = (piece, b, f, packed) + found
    return pl.pallas_call(
        functools.partial(head_kernel, nb // ZS),
        out_shape=jax.ShapeDtypeStruct((RS, nb // RS + 8, width), jnp.float32),
        in_specs=[pl.BlockSpec(memory_space=pltpu.SMEM)]
        + [pl.BlockSpec(memory_space=pltpu.VMEM)] * len(args),
        out_specs=pl.BlockSpec(memory_space=pltpu.VMEM),
        scratch_shapes=[pltpu.VMEM((nb, width), jnp.float32), pltpu.VMEM((nb, small), jnp.float32)],
        compiler_params=params(),
        cost_estimate=pl.CostEstimate(flops=10**9, bytes_accessed=0, transcendentals=0),
        name="head_terms",
    )(z, *args)


def below_kernel(group, z_ref, *refs):
    pieces, (w_ref, old_ref, new_ref) = refs[:-3], refs[-3:]
    order = (0, 1, -1, 2, -2, 3, -3, 4)
    weight = jnp.concatenate([w_ref[position(z_ref, k, group), :] for k in order], 0)
    panel = joined(pieces)
    new_ref[...] = old_ref[...] - dot3(split(panel), split(weight), ((0,), (0,)))


def below_update(z, pieces, weight, old):
    length, width = old.shape
    nb = weight.shape[0]
    return pl.pallas_call(
        functools.partial(below_kernel, nb // ZS),
        grid=(length // TILE,),
        out_shape=jax.ShapeDtypeStruct(old.shape, jnp.float32),
        in_specs=[pl.BlockSpec(memory_space=pltpu.SMEM)]
        + [pl.BlockSpec((p.shape[0], TILE), lambda i: (0, i)) for p in pieces]
        + [
            pl.BlockSpec((nb, width), lambda i: (0, 0)),
            pl.BlockSpec((TILE, width), lambda i: (i, 0)),
        ],
        out_specs=pl.BlockSpec((TILE, width), lambda i: (i, 0)),
        compiler_params=params(),
        cost_estimate=pl.CostEstimate(flops=6 * length * nb * width, bytes_accessed=0, transcendentals=0),
        name="below_update",
    )(z, *pieces, weight, old)


def finish_kernel(parts_ref, head_ref, diag_ref, new_head_ref, new_diag_ref):
    rows = head_ref.shape[0]
    small = diag_ref.shape[0]
    total = parts_ref[0]
    for r in range(1, RS):
        total = total + parts_ref[r]
    new_head_ref[...] = head_ref[...] - total[:rows]
    tail = total[rows:]
    diag = jnp.concatenate([tail[:, q * 64 : q * 64 + small] for q in range(rows // 8)], 0)
    new_diag_ref[...] = diag_ref[...] - diag.T


def finish(parts, head, diag):
    return pl.pallas_call(
        finish_kernel,
        out_shape=(
            jax.ShapeDtypeStruct(head.shape, jnp.float32),
            jax.ShapeDtypeStruct(diag.shape, jnp.float32),
        ),
        compiler_params=params(),
        name="finish",
    )(parts, head, diag)


def packed_kernel(head_ref, inverse_ref, out_ref):
    rows, width = head_ref.shape
    inverse = inverse_ref[...].T[:rows]
    for k in range(RS):
        out_ref[k, :, :width] = head_ref[...]
        out_ref[k, :, width:] = inverse


def packed_copies(head, inverse):
    rows, width = head.shape
    nb = inverse.shape[0]
    return pl.pallas_call(
        packed_kernel,
        out_shape=jax.ShapeDtypeStruct((RS, rows, width + nb), jnp.float32),
        compiler_params=params(),
        cost_estimate=pl.CostEstimate(flops=10**8, bytes_accessed=0, transcendentals=0),
        name="packed_copies",
    )(head, inverse)


def on_device(
    panel_adjoint,
    panel_factor,
    diag_inverse,
    head_factor,
    below_factor,
    diag_adjoint,
    head_adjoint,
    below_adjoint,
):
    near, far = col_groups()
    turn = 2 * (lax.axis_index("row") % 2) - 1
    z = jnp.stack([lax.axis_index("col") // YS, turn]).astype(jnp.int32)
    width = head_factor.shape[1]
    length, cols = panel_adjoint.shape
    nb = cols * ZS * YS
    group = cols * YS
    factor = panel_factor.T
    corner = jnp.pad(diag_inverse.T, ((0, 0), (0, 128 - head_factor.shape[0])))
    part = jnp.concatenate([panel_adjoint.T, corner], 1)
    part = exchange(jnp.broadcast_to(part[None], (YS,) + part.shape), "col", near)
    part = part.reshape(group, length + 128)
    inverse = jnp.broadcast_to(part[None, :, length:], (ZS, group, 128))
    inverse = exchange(inverse, "col", far).reshape(nb, 128)
    copies, later_factor = lax.optimization_barrier((packed_copies(head_factor, inverse), below_factor))
    packed = exchange(copies, "row", None).reshape(nb, width + nb)
    one = other = part[:, :length]
    pieces = [one]
    found = terms((one,), below_factor, factor, COSTS[0])
    for step in range(1, ZS // 2):
        one = lax.ppermute(one, ("row", "col"), along_z(1))
        other = lax.ppermute(other, ("row", "col"), along_z(-1))
        found += tuple(terms((one, other), later_factor, factor, COSTS[step]))
        pieces += [one, other]
    one = lax.ppermute(one, ("row", "col"), along_z(1))
    pieces.append(one)
    local = head_terms(z, one, later_factor, factor, packed, tuple(found))
    packed, local = lax.optimization_barrier((packed, local))
    weight = weights(packed, width)
    parts = lax.all_to_all(local, "row", 0, 0, tiled=True)
    below_updated = below_update(z, pieces, weight, below_adjoint)
    head_updated, diag_updated = finish(parts, head_adjoint, diag_adjoint.T)
    return (diag_updated.T, head_updated, below_updated)


def solution(mesh):
    placed = (P("row", "col"),) * 8
    return jax.shard_map(
        on_device,
        mesh=mesh,
        in_specs=placed,
        out_specs=(P("row", "col"),) * 3,
        check_vma=False,
    )
```

```python
import functools

import jax
import jax.numpy as jnp
from jax import lax
from jax.experimental import pallas as pl
from jax.experimental.pallas import tpu as pltpu
from jax.sharding import PartitionSpec as P

ZS = 8
YS = 4
RS = 16
TILE = 256
COSTS = (2 * 10**11,) * 4
VMEM = 14 * 2**20


def col_groups():
    near = [[z * YS + h for h in range(YS)] for z in range(ZS)]
    far = [[z * YS + h for z in range(ZS)] for h in range(YS)]
    return near, far


def along_z(step):
    moves = []
    for r in range(RS):
        for z in range(ZS):
            to = (z + (step if r % 2 == 0 else -step)) % ZS
            moves += [((r * ZS + z) * YS + h, (r * ZS + to) * YS + h) for h in range(YS)]
    return moves


def exchange(copies, axis, groups):
    return lax.all_to_all(copies, axis, 0, 0, tiled=True, axis_index_groups=groups)


def split(x):
    high = x.astype(jnp.bfloat16)
    return high, (x - high.astype(jnp.float32)).astype(jnp.bfloat16)


def dot3(left, right, dims):
    def one(a, b):
        return lax.dot_general(a, b, (dims, ((), ())), preferred_element_type=jnp.float32)

    return one(left[0], right[0]) + (one(left[0], right[1]) + one(left[1], right[0]))


def joined(refs):
    return jnp.concatenate([r[...] for r in refs], 0) if len(refs) > 1 else refs[0][...]


def products(pieces, b_ref, f_ref):
    piece = split(pieces)
    return dot3(piece, split(b_ref[...]), ((1,), (0,))), dot3(piece, split(f_ref[...]), ((1,), (1,)))


def term_kernel(count, *refs):
    b_ref, f_ref, t_ref, s_ref = refs[count:]
    t_ref[...], s_ref[...] = products(joined(refs[:count]), b_ref, f_ref)


def params(**more):
    return pltpu.CompilerParams(vmem_limit_bytes=VMEM, **more)


def terms(pieces, b, f, cost):
    rows = sum(p.shape[0] for p in pieces)
    return pl.pallas_call(
        functools.partial(term_kernel, len(pieces)),
        out_shape=(
            jax.ShapeDtypeStruct((rows, b.shape[1]), jnp.float32),
            jax.ShapeDtypeStruct((rows, f.shape[0]), jnp.float32),
        ),
        compiler_params=params(),
        cost_estimate=pl.CostEstimate(flops=cost, bytes_accessed=0, transcendentals=0),
        name="terms",
    )(*pieces, b, f)


def weight_kernel(packed_ref, w_ref):
    nb = packed_ref.shape[0]
    w_ref[...] = dot3(split(packed_ref[:, :nb]), split(packed_ref[:, nb:]), ((1,), (0,)))


def weights(packed, width):
    nb = packed.shape[0]
    return pl.pallas_call(
        weight_kernel,
        out_shape=jax.ShapeDtypeStruct((nb, width), jnp.float32),
        compiler_params=params(),
        cost_estimate=pl.CostEstimate(flops=10**9, bytes_accessed=0, transcendentals=0),
        name="weights",
    )(packed)


def position(z_ref, offset, group):
    place = lax.rem(z_ref[0] + offset * z_ref[1] + ZS, ZS)
    return pl.ds(pl.multiple_of(place * group, group), group)


def head_kernel(group, z_ref, *refs):
    piece_ref, b_ref, f_ref, inverse_ref = refs[:4]
    found = refs[4:12]
    out_ref, t_scr, s_scr = refs[12:]
    turned = split(inverse_ref[...].T)
    for step in range(ZS // 2):
        t_ref, s_ref = found[2 * step], found[2 * step + 1]
        for part, offset in enumerate((0,) if step == 0 else (step, -step)):
            place = position(z_ref, offset, group)
            t_scr[place, :] = t_ref[part * group : (part + 1) * group, :]
            s_scr[place, :] = s_ref[part * group : (part + 1) * group, :]
    last = position(z_ref, ZS // 2, group)
    t_scr[last, :], s_scr[last, :] = products(piece_ref[...], b_ref, f_ref)
    head = dot3(turned, split(t_scr[...]), ((1,), (0,)))
    diag = dot3(turned, split(s_scr[...]), ((1,), (0,)))
    rows = head.shape[0] // RS
    small = diag.shape[1]
    for r in range(RS):
        out_ref[r, :rows, :] = head[r * rows : (r + 1) * rows]
        for q in range(rows // 8):
            out_ref[r, rows:, q * 64 : q * 64 + small] = diag[r * rows + q * 8 : r * rows + q * 8 + 8]


def head_terms(z, piece, b, f, packed, found):
    nb = packed.shape[0]
    width, small = b.shape[1], f.shape[0]
    args = (piece, b, f, packed) + found
    return pl.pallas_call(
        functools.partial(head_kernel, nb // ZS),
        out_shape=jax.ShapeDtypeStruct((RS, nb // RS + 8, width), jnp.float32),
        in_specs=[pl.BlockSpec(memory_space=pltpu.SMEM)]
        + [pl.BlockSpec(memory_space=pltpu.VMEM)] * 3
        + [pl.BlockSpec((nb, nb), lambda i: (0, 0))]
        + [pl.BlockSpec(memory_space=pltpu.VMEM)] * len(found),
        out_specs=pl.BlockSpec(memory_space=pltpu.VMEM),
        grid=(1,),
        scratch_shapes=[pltpu.VMEM((nb, width), jnp.float32), pltpu.VMEM((nb, small), jnp.float32)],
        compiler_params=params(),
        cost_estimate=pl.CostEstimate(flops=10**9, bytes_accessed=0, transcendentals=0),
        name="head_terms",
    )(z, *args)


def below_kernel(group, z_ref, *refs):
    pieces, (w_ref, old_ref, new_ref) = refs[:-3], refs[-3:]
    order = (0, 1, -1, 2, -2, 3, -3, 4)
    weight = jnp.concatenate([w_ref[position(z_ref, k, group), :] for k in order], 0)
    panel = joined(pieces)
    new_ref[...] = old_ref[...] - dot3(split(panel), split(weight), ((0,), (0,)))


def below_update(z, pieces, weight, old):
    length, width = old.shape
    nb = weight.shape[0]
    return pl.pallas_call(
        functools.partial(below_kernel, nb // ZS),
        grid=(length // TILE,),
        out_shape=jax.ShapeDtypeStruct(old.shape, jnp.float32),
        in_specs=[pl.BlockSpec(memory_space=pltpu.SMEM)]
        + [pl.BlockSpec((p.shape[0], TILE), lambda i: (0, i)) for p in pieces]
        + [
            pl.BlockSpec((nb, width), lambda i: (0, 0)),
            pl.BlockSpec((TILE, width), lambda i: (i, 0)),
        ],
        out_specs=pl.BlockSpec((TILE, width), lambda i: (i, 0)),
        compiler_params=params(),
        cost_estimate=pl.CostEstimate(flops=6 * length * nb * width, bytes_accessed=0, transcendentals=0),
        name="below_update",
    )(z, *pieces, weight, old)


def finish_kernel(parts_ref, head_ref, diag_ref, new_head_ref, new_diag_ref):
    rows = head_ref.shape[0]
    small = diag_ref.shape[0]
    total = parts_ref[0]
    for r in range(1, RS):
        total = total + parts_ref[r]
    new_head_ref[...] = head_ref[...] - total[:rows]
    tail = total[rows:]
    diag = jnp.concatenate([tail[:, q * 64 : q * 64 + small] for q in range(rows // 8)], 0)
    new_diag_ref[...] = diag_ref[...] - diag.T


def finish(parts, head, diag):
    return pl.pallas_call(
        finish_kernel,
        out_shape=(
            jax.ShapeDtypeStruct(head.shape, jnp.float32),
            jax.ShapeDtypeStruct(diag.shape, jnp.float32),
        ),
        compiler_params=params(),
        name="finish",
    )(parts, head, diag)


def packed_kernel(head_ref, inverse_ref, out_ref):
    inverse = inverse_ref[...].T[: head_ref.shape[0]]
    nb = inverse.shape[1]
    for k in range(out_ref.shape[0]):
        out_ref[k, :, :nb] = inverse
        out_ref[k, :, nb:] = head_ref[...]


def packed_copies(head, inverse):
    rows, width = head.shape
    nb = inverse.shape[0]
    return pl.pallas_call(
        packed_kernel,
        grid=(4,),
        out_shape=jax.ShapeDtypeStruct((RS, rows, nb + width), jnp.float32),
        in_specs=[
            pl.BlockSpec(head.shape, lambda i: (0, 0)),
            pl.BlockSpec(inverse.shape, lambda i: (0, 0)),
        ],
        out_specs=pl.BlockSpec((RS // 4, rows, nb + width), lambda i: (i, 0, 0)),
        compiler_params=params(),
        cost_estimate=pl.CostEstimate(flops=10**8, bytes_accessed=0, transcendentals=0),
        name="packed_copies",
    )(head, inverse)


def on_device(
    panel_adjoint,
    panel_factor,
    diag_inverse,
    head_factor,
    below_factor,
    diag_adjoint,
    head_adjoint,
    below_adjoint,
):
    near, far = col_groups()
    turn = 2 * (lax.axis_index("row") % 2) - 1
    z = jnp.stack([lax.axis_index("col") // YS, turn]).astype(jnp.int32)
    width = head_factor.shape[1]
    length, cols = panel_adjoint.shape
    nb = cols * ZS * YS
    group = cols * YS
    factor = panel_factor.T
    corner = jnp.pad(diag_inverse.T, ((0, 0), (0, 128 - head_factor.shape[0])))
    part = jnp.concatenate([panel_adjoint.T, corner], 1)
    part = exchange(jnp.broadcast_to(part[None], (YS,) + part.shape), "col", near)
    part = part.reshape(group, length + 128)
    inverse = jnp.broadcast_to(part[None, :, length:], (ZS, group, 128))
    inverse = exchange(inverse, "col", far).reshape(nb, 128)
    copies, later_factor = lax.optimization_barrier((packed_copies(head_factor, inverse), below_factor))
    packed = exchange(copies, "row", None).reshape(nb, width + nb)
    found = {}
    ring = [part[:, :length]] * 2
    pieces = ring[:1]
    held = [ring[:1]]
    for step in range(1, ZS // 2):
        ring = [lax.ppermute(x, ("row", "col"), along_z(way)) for x, way in zip(ring, (1, -1))]
        if step > 1:
            ring[0], later_factor = lax.optimization_barrier((ring[0], later_factor))
        held.append(ring)
        pieces += ring
        if step == 2:
            found[1] = terms(held[1], later_factor, factor, COSTS[1])
            found[2] = terms(held[2], later_factor, factor, COSTS[2])
        if step == 3:
            found[0] = terms(held[0], later_factor, factor, COSTS[0])
            found[3] = terms(held[3], later_factor, factor, COSTS[3])
    one = lax.ppermute(ring[0], ("row", "col"), along_z(1))
    pieces.append(one)
    found = [x for step in range(ZS // 2) for x in found[step]]
    local = head_terms(z, one, later_factor, factor, packed, tuple(found))
    packed, local = lax.optimization_barrier((packed, local))
    weight = weights(packed, width)
    parts = lax.all_to_all(local, "row", 0, 0, tiled=True)
    below_updated = below_update(z, pieces, weight, below_adjoint)
    head_updated, diag_updated = finish(parts, head_adjoint, diag_adjoint.T)
    return (diag_updated.T, head_updated, below_updated)


def solution(mesh):
    placed = (P("row", "col"),) * 8
    return jax.shard_map(
        on_device,
        mesh=mesh,
        in_specs=placed,
        out_specs=(P("row", "col"),) * 3,
        check_vma=False,
    )
```
